32 devices in a mesh: img: 8 (over y, x, core), row: 4 (over z).
Axes of the slice: x: 2, y: 2, z: 4, core: 2. Of those that a mesh axis runs over, the one named last changes fastest.
Arguments:
- images: bfloat16 [8, 20, 96, 512], P('img', 'row'), may hold values from -6 to 6
- cotangent: bfloat16 [8, 20, 96, 512], P('img', 'row'), may hold values from -6 to 6
- params: bfloat16 [2, 3111680], P(None, ('img', 'row')), may hold values from -2 to 2, as said below
- heights: int32 [8], P('img'), may hold values from 18 to 20, as said below
- widths: int32 [8], P('img'), may hold values from 48 to 96, as said below
Outputs:
- outputs: bfloat16 [8, 20, 96, 512], P('img', 'row')
- input_grad: bfloat16 [8, 20, 96, 512], P('img', 'row')
- param_grads: float32 [2, 3111680], P(None, ('img', 'row'))
The draws below stay inside these ranges and needn't reach their ends.
Inputs may be any that keep to these rules, and one draw needn't show every extreme that they name: `params`: zero in each block's padding beyond 3111680. `heights`: one image has all 20 rows and one has 18. `widths`: one image has all 96 columns and one has 48.
All inputs are finite; a program needn't handle non-finite values.
Results may differ from the reference program's by a relative error of at most 0.025.
Values may be sent and summed in bfloat16 or wider, within the bound.
A program may use at most 192 MiB of HBM per device.

```python
import math
import jax
import jax.numpy as jnp
from jax import lax

D = 512
RS = 5
W = 96
LAYERS = 2
H = 20
IMAGES = 8
PARAMS = 3111680


def layout_drawn(width):
    first = width // 8
    mixed = 15 * width // 8
    return [('norm_gain', (width,)), ('norm_shift', (width,)), ('inner_weight', (width, 2 * width)), ('inner_bias', (2 * width,)), ('kernel', (7, 7, mixed)), ('kernel_bias', (mixed,)), ('order_one', (first, 2 * first)), ('bias_one', (2 * first,)), ('order_two', (2 * first, 4 * first)), ('bias_two', (4 * first,)), ('order_three', (4 * first, 8 * first)), ('bias_three', (8 * first,)), ('outer_weight', (width, width)), ('outer_bias', (width,)), ('scale_mixer', (width,)), ('second_gain', (width,)), ('second_shift', (width,)), ('expand', (width, 4 * width)), ('expand_bias', (4 * width,)), ('reduce', (4 * width, width)), ('reduce_bias', (width,)), ('scale_mlp', (width,))]


def segment_law(width):
    table = []
    offset = 0
    for name, shape in layout_drawn(width):
        count = math.prod(shape)
        if name in ('norm_gain', 'second_gain', 'scale_mixer', 'scale_mlp'):
            middle, spread = (1.0, 0.2)
        elif len(shape) == 1:
            middle, spread = (0.0, 0.2)
        elif name == 'kernel':
            middle, spread = (0.0, 3.0 / 7.0)
        else:
            middle, spread = (0.0, shape[0] ** (-0.5))
        table.append((offset, offset + count, middle, spread))
        offset = offset + count
    return table


def draw_params(key, part):
    key = jax.random.fold_in(key, 5)
    noise = jnp.clip(jax.random.normal(key, (LAYERS, PARAMS), jnp.float32), -4.0, 4.0)
    index = jnp.arange(PARAMS)
    center = jnp.zeros((PARAMS,), jnp.float32)
    spread = jnp.zeros((PARAMS,), jnp.float32)
    for start, stop, middle, scale in segment_law(D):
        inside = (index >= start) & (index < stop)
        center = jnp.where(inside, middle, center)
        spread = jnp.where(inside, scale, spread)
    return (center + spread * noise).astype(jnp.bfloat16)


def ragged_extent(key, largest, smallest):
    chosen, values_key = jax.random.split(key)
    order = jax.random.permutation(chosen, IMAGES)
    drawn = jax.random.randint(values_key, (IMAGES,), smallest, largest + 1)
    drawn = jnp.where(order == 0, largest, drawn)
    drawn = jnp.where(order == 1, smallest, drawn)
    return drawn.astype(jnp.int32)


def draw_heights(key, part):
    key = jax.random.fold_in(key, 11)
    return ragged_extent(key, H, H - RS // 2)


def draw_widths(key, part):
    key = jax.random.fold_in(key, 17)
    return ragged_extent(key, W, W // 2)


def shard_levels(own_key, shape, cuts, low, high):
    level = 1.0
    for position, shards_of in cuts:
        draws = jax.random.uniform(jax.random.fold_in(jax.random.fold_in(own_key, 6), position), (shards_of,), jnp.float32, low / len(cuts), high / len(cuts))
        level = level * jnp.repeat(jnp.exp(draws), shape[position] // shards_of).reshape((-1,) + (1,) * (len(shape) - 1 - position))
    return level


def centred(own_key, extent, deviation, bound, cuts=(), kind=jnp.bfloat16):
    entries = deviation * jax.random.normal(own_key, extent, jnp.float32)
    if cuts:
        entries = entries * shard_levels(own_key, extent, cuts, -0.22, 0.18)
    return jnp.clip(entries, -bound, bound).astype(kind)


def setup_inputs(seed: int = 0) -> dict:
    key_of = jax.random.split(jax.random.key(seed), 6)
    return {
        "images": centred(key_of[0], (IMAGES, H, W, D), 1.0, 6.0, ((0, 8), (1, 4))),
        "cotangent": centred(key_of[1], (IMAGES, H, W, D), 1.0, 6.0, ((0, 8), (1, 4))),
        "params": draw_params(jax.random.fold_in(key_of[5], 71), 0),
        "heights": draw_heights(jax.random.fold_in(key_of[5], 71), 0),
        "widths": draw_widths(jax.random.fold_in(key_of[5], 71), 0),
    }


@jax.custom_vjp
def low(v):
    return lax.optimization_barrier(v.astype(jnp.bfloat16)).astype(jnp.float32)

@jax.custom_vjp
def low_back(v):
    return v

def low_keep(v):
    return (low(v), None)

def low_pass(kept, grad):
    return (grad,)

def back_keep(v):
    return (v, None)

def back_low(kept, grad):
    return (low(grad),)
low.defvjp(low_keep, low_pass)
low_back.defvjp(back_keep, back_low)
HIGHEST = lax.Precision.HIGHEST
THIRD = 1.0 / 3.0

def layout(width):
    first = width // 8
    mixed = 15 * width // 8
    return [('norm_gain', (width,)), ('norm_shift', (width,)), ('inner_weight', (width, 2 * width)), ('inner_bias', (2 * width,)), ('kernel', (7, 7, mixed)), ('kernel_bias', (mixed,)), ('order_one', (first, 2 * first)), ('bias_one', (2 * first,)), ('order_two', (2 * first, 4 * first)), ('bias_two', (4 * first,)), ('order_three', (4 * first, 8 * first)), ('bias_three', (8 * first,)), ('outer_weight', (width, width)), ('outer_bias', (width,)), ('scale_mixer', (width,)), ('second_gain', (width,)), ('second_shift', (width,)), ('expand', (width, 4 * width)), ('expand_bias', (4 * width,)), ('reduce', (4 * width, width)), ('reduce_bias', (width,)), ('scale_mlp', (width,))]

def unpack(flat, width):
    pieces = {}
    offset = 0
    for name, shape in layout(width):
        count = math.prod(shape)
        pieces[name] = flat[offset:offset + count].reshape(shape)
        offset = offset + count
    return pieces

def matmul(left, right):
    return jnp.dot(left, right, precision=HIGHEST, preferred_element_type=jnp.float32)

def normalize(values, gain, shift):
    mean = lax.optimization_barrier(jnp.mean(values, -1, keepdims=True))
    centered = values - mean
    return centered * lax.rsqrt(lax.optimization_barrier(jnp.mean(centered * centered, -1, keepdims=True)) + 1e-06) * gain + shift

def depthwise(field, kernel):
    rows, cols = (field.shape[0], field.shape[1])
    padded = jnp.pad(field, ((3, 3), (3, 3), (0, 0)))
    total = jnp.zeros_like(field)
    for row in range(7):
        for col in range(7):
            total = total + padded[row:row + rows, col:col + cols] * kernel[row, col]
    return total

def block(values, weights, valid):
    width = values.shape[-1]
    first = width // 8
    normed = low(normalize(values, weights['norm_gain'], weights['norm_shift']))
    inner = low_back(matmul(normed, weights['inner_weight']) + weights['inner_bias'])
    rest = low(inner[..., first:] * valid[..., None])
    mixed = low_back(depthwise(rest, weights['kernel']) + weights['kernel_bias']) * THIRD
    gated = inner[..., :first] * mixed[..., :first]
    start = first
    for name, bias in (('order_one', 'bias_one'), ('order_two', 'bias_two'), ('order_three', 'bias_three')):
        size = weights[name].shape[1]
        gated = low_back(matmul(low(gated), weights[name]) + weights[bias]) * mixed[..., start:start + size]
        start = start + size
    branch = low_back(matmul(low(gated), weights['outer_weight']) + weights['outer_bias'])
    middle = values + weights['scale_mixer'] * branch
    normed = low(normalize(middle, weights['second_gain'], weights['second_shift']))
    hidden = low_back(matmul(normed, weights['expand']) + weights['expand_bias'])
    active = low(jax.nn.gelu(hidden, approximate=False))
    branch = low_back(matmul(active, weights['reduce']) + weights['reduce_bias'])
    return middle + weights['scale_mlp'] * branch

def reference(images, cotangent, params, heights, widths):
    weights = params.astype(jnp.float32)
    rows = jnp.arange(H, dtype=jnp.int32)
    cols = jnp.arange(W, dtype=jnp.int32)

    def one_image(totals, inputs):
        picture, upstream, height, width = inputs
        valid = ((rows[:, None] < height) & (cols[None, :] < width)).astype(jnp.float32)

        def forward(values, flat):
            for layer in range(LAYERS):
                values = block(values, unpack(flat[layer], D), valid)
            return values
        result, pullback = jax.vjp(forward, picture.astype(jnp.float32), weights)
        back_input, back_weights = pullback(upstream.astype(jnp.float32))
        return (totals + back_weights, (result.astype(jnp.bfloat16), back_input.astype(jnp.bfloat16)))
    totals, (outputs, grads) = lax.scan(one_image, jnp.zeros_like(weights), (images, cotangent, heights, widths))
    return (outputs, grads, totals)
```

```python
import functools
import math
from types import SimpleNamespace

import jax
import jax.numpy as jnp
from jax import lax
from jax.experimental import pallas as pl
from jax.experimental.pallas import tpu as pltpu
from jax.sharding import PartitionSpec as P

BF = jnp.bfloat16
F32 = jnp.float32
THIRD = 1.0 / 3.0
LANES = 128
TILE = 16
UNIT = TILE * LANES
NT = (((1,), (1,)), ((), ()))
TN = (((0,), (0,)), ((), ()))
MESH = pl.DeviceIdType.MESH
LINK, HOP = 75e3, 3.2
LAST_LINK, LAST_HOP = 65e3, 4.0
VMEM_LIMIT = 62 * 1024 * 1024 + 512 * 1024
WIDTH = 512


def layout(width):
    first = width // 8
    mixed = 15 * width // 8
    return [
        ("norm_gain", (width,)),
        ("norm_shift", (width,)),
        ("inner_weight", (width, 2 * width)),
        ("inner_bias", (2 * width,)),
        ("kernel", (7, 7, mixed)),
        ("kernel_bias", (mixed,)),
        ("order_one", (first, 2 * first)),
        ("bias_one", (2 * first,)),
        ("order_two", (2 * first, 4 * first)),
        ("bias_two", (4 * first,)),
        ("order_three", (4 * first, 8 * first)),
        ("bias_three", (8 * first,)),
        ("outer_weight", (width, width)),
        ("outer_bias", (width,)),
        ("scale_mixer", (width,)),
        ("second_gain", (width,)),
        ("second_shift", (width,)),
        ("expand", (width, 4 * width)),
        ("expand_bias", (4 * width,)),
        ("reduce", (4 * width, width)),
        ("reduce_bias", (width,)),
        ("scale_mlp", (width,)),
    ]


def chunk_table():
    table, offset = {}, 0
    for name, shape in layout(WIDTH):
        table[name] = (offset // LANES, shape)
        offset += math.prod(shape)
    return table, offset


CHUNK, USED = chunk_table()
CHUNKS = USED // LANES
BODY_ROWS = -(-CHUNKS // 256) * 256
FLAT_ROWS = BODY_ROWS + 256
SPLIT = CHUNK["order_one"][0]
PART = -(-(SPLIT + 1) // TILE) * TILE
MIDDLE = BODY_ROWS - 16384
PLACE = {name: start for name, (start, _) in CHUNK.items()}
MOVED = {"expand_bias": (16080, 7904), "reduce_bias": (24288, 7936), "scale_mlp": (24288, 7936)}
for _name, (_from, _to) in MOVED.items():
    PLACE[_name] += _to - _from
KEPT_ROWS = 8192
TILES = [(row, row, 0, 16) for row in range(CHUNK["kernel"][0], PART, TILE)] + [
    (0, 0, 0, 8),
    (4096, 4096, 8, 16),
    (7904, 16080, 14, 16),
    (7920, 16096, 0, 14),
    (7936, 24288, 14, 16),
    (7952, 24304, 0, 6),
]
WIRED = ("reduce", "expand", "inner_weight")
GATES_END = CHUNK["expand"][0]
VECTORS = [
    name
    for name, shape in layout(WIDTH)
    if len(shape) == 1 and name != "kernel_bias"
]
MATRICES = [name for name, shape in layout(WIDTH) if len(shape) == 2]
PADDED = {name: CHUNK[name][1] for name in MATRICES}
PADDED["order_one"] = (LANES, LANES)


def lanes(index, size):
    return pl.ds(pl.multiple_of(index * size, size), size)


def loop(count, body):
    def step(index, carry):
        body(index)
        return carry

    lax.fori_loop(0, count, step, 0)


def column_sum(value):
    return jnp.sum(value.astype(F32), axis=0, keepdims=True)


def normal_of(values):
    mean = jnp.mean(values, -1, keepdims=True)
    centered = values - mean
    inverse = lax.rsqrt(jnp.mean(centered * centered, -1, keepdims=True) + 1e-06)
    return centered * inverse, inverse


def norm_back(grad_normed, normal, inverse, gain):
    scaled = grad_normed * gain
    return inverse * (
        scaled
        - jnp.mean(scaled, -1, keepdims=True)
        - normal * jnp.mean(scaled * normal, -1, keepdims=True)
    )


def product(left, right, dims=None):
    if dims is None:
        return jnp.dot(left, right, preferred_element_type=F32)
    return lax.dot_general(left, right, dims, preferred_element_type=F32)


def half_mask(rows):
    return lax.broadcasted_iota(jnp.int32, (rows, LANES), 1) < LANES // 2


def taps_from_flat(flat, taps, bias):
    low = half_mask(8)
    top = lax.broadcasted_iota(jnp.int32, (8, LANES), 0) == 0
    start = CHUNK["kernel"][0]

    def keep(tap, value):
        taps[8 * tap : 8 * tap + 8, :] = value

    for pair in range(25):
        base = start + 15 * pair
        even = pltpu.roll(flat[base : base + 8, :], LANES // 2, 1)
        down = pltpu.roll(even, 1, 0)
        keep(2 * pair, jnp.where(low, jnp.where(top, 0.0, down), even))
        odd = jnp.where(low & top, 0.0, flat[base + 7 : base + 15, :])
        if pair == 24:
            bias[...] = odd
        else:
            keep(2 * pair + 1, odd)


def taps_to_flat(taps, flat):
    low = half_mask(8)
    top = lax.broadcasted_iota(jnp.int32, (8, LANES), 0) == 0
    start = CHUNK["kernel"][0]
    for pair in range(25):
        base = start + 15 * pair
        even = pltpu.roll(taps[16 * pair : 16 * pair + 8, :], LANES // 2, 1)
        up = pltpu.roll(even, 7, 0)
        odd = taps[16 * pair + 8 : 16 * pair + 16, :]
        flat[base : base + 8, :] = jnp.where(low, even, up)
        last = pltpu.roll(even, 1, 0)
        flat[base + 7 : base + 15, :] = jnp.where(low & top, last, odd)


def weights_from_flat(flat, weights, vectors, taps, bias, beside):
    for name in MATRICES:
        start, (depth, width) = CHUNK[name]
        count = width // LANES
        block = min(depth, 256)
        target = getattr(weights, name)
        for tile in range(count):

            def move(index, tile=tile):
                row = pl.multiple_of(index * block, block)
                if count == 1:
                    source = pl.ds(start, block)
                else:
                    source = pl.ds(start + tile + row * count, block, stride=count)
                target[pl.ds(row, block), tile * LANES : (tile + 1) * LANES] = flat[
                    source, :
                ].astype(BF)

            if depth == block:
                move(0)
            else:
                loop(depth // block, move)
        beside.tick(depth * width * 1.6e-6)
    weights.order_one[LANES // 2 :, :] = jnp.zeros((LANES // 2, LANES), BF)
    for index, name in enumerate(VECTORS):
        start, (width,) = CHUNK[name]
        for tile in range(width // LANES):
            vectors[index : index + 1, tile * LANES : (tile + 1) * LANES] = flat[
                start + tile : start + tile + 1, :
            ]
    taps_from_flat(flat, taps, bias)


class Vectors:
    def __init__(self, ref):
        self.ref = ref

    def __getattr__(self, name):
        index = VECTORS.index(name)
        return self.ref[index : index + 1, : CHUNK[name][1][0]]

    def part(self, name, tile, size):
        index = VECTORS.index(name)
        return self.ref[index : index + 1, lanes(tile, size)]


def store_vector(flat, name, value, tile=0):
    count = value.shape[1] // LANES
    start = PLACE[name] + tile * count
    for index in range(count):
        flat[pl.ds(start + index, 1), :] = value[:, index * LANES : (index + 1) * LANES]


def store_matrix(r, name, value, row=0, tile=0):
    if name in r.wires:
        count = value.shape[1] // LANES
        for index in range(count):
            part = value[:, index * LANES : (index + 1) * LANES].astype(BF)
            r.wires[name][tile * count + index, pl.ds(row, value.shape[0]), :] = part
        return
    flat = r.flat
    start, (depth, width) = CHUNK[name]
    count = width // LANES
    rows = value.shape[0]
    for index in range(value.shape[1] // LANES):
        first = start + row * count + tile * (value.shape[1] // LANES) + index
        if count == 1:
            flat[pl.ds(first, rows), :] = value
        else:
            flat[pl.ds(first, rows, stride=count), :] = value[
                :, index * LANES : (index + 1) * LANES
            ]


class Grid:
    def __init__(self, rows, cols):
        self.rows, self.cols = rows, cols
        self.pixels = rows * cols
        self.tall, self.wide = rows + 6, cols + 6
        self.halo = 3 * cols
        self.all = self.tall * cols
        self.step = 12
        self.blocks = cols // self.step
        self.taps_step = 12
        self.taps_blocks = cols // (2 * self.taps_step)

    def at(self, row, place):
        return (row * self.wide + place) * 8


def register(ref, index):
    return ref[pl.ds(pl.multiple_of(index, 8), 8), :]


def tree(terms):
    while len(terms) > 1:
        left = terms[len(terms) // 2 * 2 :]
        terms = [a + b for a, b in zip(terms[::2], terms[1::2])] + left
    return terms[0]


def depthwise(grid, field, taps, target, flip, finish, beside):
    def block_at(row, block):
        base = grid.at(row, block * grid.step)
        sums = [None] * grid.step
        for i in range(7):
            line = [
                register(field, base + grid.at(i, q)) for q in range(grid.step + 6)
            ]
            for j in range(7):
                tap = 7 * i + j
                tap = 48 - tap if flip else tap
                weight = taps[tap * 8 : tap * 8 + 8, :]
                for c in range(grid.step):
                    term = line[c + j] * weight
                    sums[c] = term if sums[c] is None else sums[c] + term
        first = (row * grid.cols + block * grid.step) * 8
        for c in range(grid.step):
            target[pl.ds(pl.multiple_of(first + c * 8, 8), 8), :] = finish(sums[c])

    pairs = grid.blocks // 2

    def body(index):
        row, pair = index // pairs, index % pairs
        block_at(row, 2 * pair)
        block_at(row, 2 * pair + 1)
        beside.inside(index, grid.rows * pairs, 10, 12.0)

    loop(grid.rows * pairs, body)


def depthwise_taps(grid, field, grads, target, beside, first, last):
    step, blocks = grid.taps_step, grid.taps_blocks

    def per_row(i):
        def body(index, sums):
            row, block = index // blocks, index % blocks
            for part in range(2):
                col = (2 * block + part) * step
                start = grid.at(row + 3, col + 3)
                grad = [register(grads, start + 8 * c) for c in range(step)]
                base = grid.at(row + i, col)
                line = [register(field, base + 8 * q) for q in range(step + 6)]
                sums = tuple(
                    sums[j] + tree([line[c + j] * grad[c] for c in range(step)]) for j in range(7)
                )
            return sums

        zero = jnp.zeros((8, LANES), F32)
        sums = lax.fori_loop(0, grid.rows * blocks, body, (zero,) * 7)
        for j in range(7):
            target[pl.ds(pl.multiple_of((i * 7 + j) * 8, 8), 8), :] = sums[j]
        beside.inside(i - first, last - first, last - first, 1.7 * (last - first))

    loop(last - first, lambda index: per_row(index + first))


def to_field(grid, source, field, first, count):
    zero = jnp.zeros((24, LANES), F32)

    def per_row(row):
        rows = lanes(row, grid.cols)
        base = grid.at(first + row, 0)
        field[pl.ds(pl.multiple_of(base, 8), 24), :] = zero
        field[pl.ds(pl.multiple_of(base + (grid.cols + 3) * 8, 8), 24), :] = zero
        for tile in range(8):
            value = source[rows, tile * LANES : (tile + 1) * LANES].astype(F32)
            field[pl.ds(base + 24 + tile, grid.cols, stride=8), :] = value

    loop(count, per_row)


def gelu_parts(hidden):
    half = 0.5 * (1.0 + lax.erf(hidden * (1.0 / math.sqrt(2.0))))
    bell = jnp.exp(hidden * hidden * -0.5) * (1.0 / math.sqrt(2.0 * math.pi))
    return hidden * half, half + hidden * bell


LINE_AT = {1: (0, 128), 2: (128, 256), 3: (384, 512)}
GATE_AT = {0: (0, 128), 1: (128, 128), 2: (256, 256), 3: (512, 512)}
ORDER = {1: "order_one", 2: "order_two", 3: "order_three"}
SECOND = ("second_gain", "second_shift", "scale_mixer", "outer_bias")
ENDS = "ends"
CREDIT, SOURCE, BEFORE, DASH = "credit", "source_{}", "before_{}", "_"
SUMS, SENDS, RECEIVES = "sums_{}_{}_{}", "sends_{}_{}", "receives_{}_{}"
BIAS = {1: "bias_one", 2: "bias_two", 3: "bias_three"}


def mixed_tiles(grid, mixed, first, count):
    parts = [
        mixed[pl.ds(first + t, grid.pixels, stride=8), :] for t in range(count)
    ]
    return parts[0] if count == 1 else jnp.concatenate(parts, axis=1)


class Steps:
    def __init__(self, pace=(LINK, HOP)):
        self.waiting, self.clock, self.pace = [], 0.0, pace

    def add(self, steps):
        self.waiting += [(self.clock + time, step) for time, step in steps]
        self.waiting.sort(key=lambda item: item[0])

    def due(self, time):
        self.clock += time
        now = [step for ready, step in self.waiting if ready <= self.clock]
        self.waiting = self.waiting[len(now) :]
        return now

    def tick(self, time):
        for step in self.due(time):
            step()

    def inside(self, index, count, parts, time):
        period = count // parts
        places = [(part * period, self.due(time / parts)) for part in range(parts)]
        places = [(place, steps) for place, steps in places if steps]

        def run(steps):
            for step in steps:
                step()

        def some():
            for place, steps in places:
                pl.when(index == place)(functools.partial(run, steps))

        if places and period > 1:
            pl.when(index % period == 0)(some)
        elif places:
            some()

    def drain(self, between=lambda: None):
        ends = [step for _, step in self.waiting if hasattr(step, ENDS)]
        for _, step in self.waiting:
            if not hasattr(step, ENDS):
                step()
        for step in ends[:-2]:
            step()
        between()
        for step in ends[-2:]:
            step()
        self.waiting = []


def forward(grid, w, v, taps, r, beside, halo_here, written):
    own = (r.x, 3, grid.rows)
    parts = (own, (r.x_up, 0, 3), (r.x_down, 3 + grid.rows, 3))
    gain, shift = v.norm_gain, v.norm_shift
    for source, first, count in parts:

        def norm_row(index, source=source, first=first):
            rows = lanes(index, grid.cols)
            normal, _ = normal_of(source[rows, :].astype(F32))
            r.normed_all[lanes(index + first, grid.cols), :] = (
                normal * gain + shift
            ).astype(BF)

        loop(count, norm_row)
        if first == 3:
            halo_here()
        beside.tick(0.6)

    side = pl.ds(0, grid.halo)
    rest = {
        0: r.active.at[side, pl.ds(0, 2 * WIDTH)],
        3: r.gated,
        3 + grid.rows: r.active.at[side, pl.ds(2 * WIDTH, 2 * WIDTH)],
    }

    def inner_tile(tile):
        columns = lanes(tile, 256)
        weight = w.inner_weight[:, columns]
        bias = v.part("inner_bias", tile, 256)
        for _, first, count in parts:
            rows = slice(first * grid.cols, (first + count) * grid.cols)
            inner = product(r.normed_all[rows, :], weight) + bias
            if first == 3:

                @pl.when(tile == 0)
                def _():
                    r.head[...] = inner[:, :LANES]

            valid = r.mask[rows, :] > 0.0
            valid = jnp.concatenate([valid, valid], axis=1)
            rest[first][:, columns] = jnp.where(valid, inner, 0.0).astype(BF)
        beside.inside(tile, 4, 4, 2.0)

    loop(2 * WIDTH // 256, inner_tile)
    for _, first, count in parts:
        to_field(grid, rest[first], r.field, first, count)
        beside.tick(0.5)
    written()

    bias = r.bias[...]
    depthwise(
        grid, r.field, taps, r.mixed, False, lambda s: (s + bias) * THIRD, beside
    )

    low = half_mask(grid.pixels)
    first_gate = pltpu.roll(mixed_tiles(grid, r.mixed, 0, 1), LANES // 2, 1)
    gated = jnp.where(low, r.head[...] * first_gate, 0.0)
    r.gated[:, :LANES] = gated.astype(BF)
    for k in (1, 2, 3):
        at, size = GATE_AT[k - 1]
        low_gated = r.gated[:, at : at + size]
        at, size = LINE_AT[k]
        for tile in range(max(size // 256, 1)):
            part = min(size, 256)
            inside = slice(tile * part, (tile + 1) * part)
            line = product(low_gated, getattr(w, ORDER[k])[:, inside]) + getattr(v, BIAS[k])[:, inside]
            r.lines[:, at + tile * part : at + (tile + 1) * part] = line.astype(BF)
            start = GATE_AT[k][0] + tile * part
            gate = mixed_tiles(grid, r.mixed, start // LANES, part // LANES)
            r.gated[:, start : start + part] = (line * gate).astype(BF)
        beside.tick(0.7)

    def outer_tile(tile):
        columns = lanes(tile, 256)
        branch = product(r.gated[:, 512:], w.outer_weight[:, columns]) + v.part(
            "outer_bias", tile, 256
        )
        r.branch_a[:, columns] = branch.astype(BF)
        r.middle[:, columns] = (
            r.x[:, columns].astype(F32) + v.part("scale_mixer", tile, 256) * branch
        )

    loop(WIDTH // 256, outer_tile)
    beside.tick(0.7)
    gain, shift = v.second_gain, v.second_shift

    def second_norm(index):
        rows = lanes(index, grid.cols)
        normal, _ = normal_of(r.middle[rows, :])
        r.normed_b[rows, :] = (normal * gain + shift).astype(BF)

    loop(grid.rows, second_norm)
    beside.tick(0.6)
    written()

    def expand_tile(tile):
        columns = lanes(tile, 256)
        hidden = product(r.normed_b[...], w.expand[:, columns]) + v.part(
            "expand_bias", tile, 256
        )
        active, slope = gelu_parts(hidden)
        r.active[:, columns] = active.astype(BF)
        r.slope[:, columns] = slope.astype(BF)

    def expand_pair(index):
        expand_tile(2 * index)
        expand_tile(2 * index + 1)
        beside.inside(index, 4, 4, 5.0)

    loop(4, expand_pair)
    written()

    def reduce_tile(tile):
        columns = lanes(tile, 256)
        branch = product(r.active[...], w.reduce[:, columns]) + v.part(
            "reduce_bias", tile, 256
        )
        r.branch_b[:, columns] = branch.astype(BF)
        result = r.middle[:, columns] + v.part("scale_mlp", tile, 256) * branch
        r.result[:, columns] = result
        beside.inside(tile, 2, 2, 1.0)

    loop(WIDTH // 256, reduce_tile)
    written()


def backward_one(grid, w, v, r, flat, beside, needed, halfway, expanded, widest_here):
    def reduce_in(tile):
        columns = lanes(tile, 256)
        grad = r.grad[:, columns].astype(F32)
        store_vector(flat, "scale_mlp", column_sum(grad * r.branch_b[:, columns].astype(F32)), tile)
        low = (grad * v.part("scale_mlp", tile, 256)).astype(BF)
        r.low[:, columns] = low
        store_vector(flat, "reduce_bias", column_sum(low), tile)

    loop(WIDTH // 256, reduce_in)
    needed()
    r.turned[...] = r.normed_b[...].T
    beside.tick(1.0)

    def expand_tile(tile):
        columns = lanes(tile, 256)
        store_matrix(
            r, "reduce", product(r.active[:, columns], r.low[...], TN), row=tile * 256
        )
        active = product(r.low[...], w.reduce[columns, :], NT)
        hidden = (active * r.slope[:, columns].astype(F32)).astype(BF)
        r.slope[:, columns] = hidden
        store_vector(flat, "expand_bias", column_sum(hidden), tile)
        store_matrix(r, "expand", product(r.turned[...], hidden), tile=tile)

    def expand_pair(index, first):
        expand_tile(2 * index + first)
        expand_tile(2 * index + first + 1)
        beside.inside(index, 2, 2, 3.7)

    loop(2, lambda index: expand_pair(index, 0))
    halfway()
    loop(2, lambda index: expand_pair(index, 4))
    expanded()
    needed()

    def expand_in(tile):
        columns = lanes(tile, 256)
        r.wide[:, columns] = product(r.slope[...], w.expand[columns, :], NT)

    loop(WIDTH // 256, expand_in)
    beside.tick(1.2)
    gain, scale = v.second_gain, v.scale_mixer

    def second_back(index, sums):
        rows = lanes(index, grid.cols)
        normal, inverse = normal_of(r.middle[rows, :])
        grad = r.wide[rows, :]
        back = r.grad[rows, :].astype(F32) + norm_back(grad, normal, inverse, gain)
        branch = r.branch_a[rows, :].astype(F32)
        r.back[rows, :] = back
        low = (back * scale).astype(BF)
        r.low[rows, :] = low
        return (
            sums[0] + column_sum(grad * normal),
            sums[1] + column_sum(grad),
            sums[2] + column_sum(back * branch),
            sums[3] + column_sum(low),
        )

    zero = jnp.zeros((1, WIDTH), F32)
    sums = lax.fori_loop(0, grid.rows, second_back, (zero,) * 4)
    for name, value in zip(SECOND, sums):
        store_vector(flat, name, value)
    beside.tick(1.0)
    needed()

    r.turned[...] = r.gated[:, 512:].T

    def outer_tile(tile):
        columns = lanes(tile, 256)
        store_matrix(
            r, "outer_weight", product(r.turned[...], r.low[:, columns]), tile=tile
        )
        r.wide[:, columns] = product(r.low[...], w.outer_weight[columns, :], NT)

    loop(WIDTH // 256, outer_tile)
    beside.tick(1.2)

    for k in (3, 2, 1):
        at, size = LINE_AT[k]
        start = GATE_AT[k][0]
        part = min(size, 256)
        for tile in range(size // part):
            inside = slice(tile * part, (tile + 1) * part)
            grad = r.wide[:, inside]
            gate = mixed_tiles(grid, r.mixed, (start + tile * part) // LANES, part // LANES)
            low = (grad * gate).astype(BF)
            r.low[:, inside] = low
            store_vector(flat, BIAS[k], column_sum(low), tile)
            dm = grad * r.lines[:, at + tile * part : at + (tile + 1) * part].astype(F32)
            r.gated[:, start + tile * part : start + (tile + 1) * part] = (dm * THIRD).astype(BF)
        before, depth = GATE_AT[k - 1]
        grad = product(r.gated[:, before : before + depth], r.low[:, :size], TN)
        store_matrix(r, ORDER[k], grad[: CHUNK[ORDER[k]][1][0], :])
        r.wide[:, :depth] = product(r.low[:, :size], getattr(w, ORDER[k])[...], NT)
        if k == 3:
            widest_here()
        beside.tick(1.3)

    low = half_mask(grid.pixels)
    grad = r.wide[:, :LANES]
    first_gate = pltpu.roll(mixed_tiles(grid, r.mixed, 0, 1), LANES // 2, 1)
    dm = pltpu.roll(grad * r.head[...], LANES // 2, 1)
    r.head[...] = grad * first_gate
    r.gated[:, :LANES] = jnp.where(low, 0.0, dm * THIRD).astype(BF)


def backward_two(grid, w, v, taps, r, flat, beside, needed, halo_here, inner_here, before):
    needed()
    to_field(grid, r.gated, r.grads, 3, grid.rows)
    beside.tick(0.8)
    depthwise_taps(grid, r.field, r.grads, r.taps_grad, beside, 0, before)
    halo_here()
    to_field(grid, r.grad_up, r.grads, 0, 3)
    to_field(grid, r.grad_down, r.grads, 3 + grid.rows, 3)
    beside.tick(1.5)
    depthwise(grid, r.grads, taps, r.mixed, True, lambda s: s, beside)
    low = half_mask(grid.cols)
    for row in range(grid.rows):
        rows = slice(row * grid.cols, (row + 1) * grid.cols)
        valid = r.mask_own[rows, :] > 0.0
        for tile in range(8):
            value = r.mixed[pl.ds(row * grid.cols * 8 + tile, grid.cols, stride=8), :]
            value = jnp.where(valid, value, 0.0)
            if tile == 0:
                value = jnp.where(low, r.head[rows, :], value)
            r.active[rows, tile * LANES : (tile + 1) * LANES] = value.astype(BF)
    beside.tick(0.8)

    r.turned[...] = r.normed[...].T

    def inner_tile(tile):
        columns = lanes(tile, 256)
        grad = r.active[:, columns]
        store_vector(flat, "inner_bias", column_sum(grad), tile)
        store_matrix(r, "inner_weight", product(r.turned[...], grad), tile=tile)
        beside.inside(tile, 4, 4, 2.5)

    loop(2 * WIDTH // 256, inner_tile)
    inner_here()
    if before < 7:
        depthwise_taps(grid, r.field, r.grads, r.taps_grad, beside, before, 7)
    for tile in range(8):
        value = r.gated[:, tile * LANES : (tile + 1) * LANES]
        r.taps_grad[49 * 8 + tile : 49 * 8 + tile + 1, :] = column_sum(value)
    taps_to_flat(r.taps_grad, flat)

    def first_tile(tile):
        columns = lanes(tile, 256)
        r.wide[:, columns] = product(r.active[:, : 2 * WIDTH], w.inner_weight[columns, :], NT)

    loop(WIDTH // 256, first_tile)
    beside.tick(0.8)
    gain = v.norm_gain

    def first_back(index, sums):
        rows = lanes(index, grid.cols)
        normal, inverse = normal_of(r.x[rows, :].astype(F32))
        grad = r.wide[rows, :]
        result = r.back[rows, :] + norm_back(grad, normal, inverse, gain)
        r.input_grad[rows, :] = result.astype(r.input_grad.dtype)
        return (sums[0] + column_sum(grad * normal), sums[1] + column_sum(grad))

    zero = jnp.zeros((1, WIDTH), F32)
    sums = lax.fori_loop(0, grid.rows, first_back, (zero,) * 2)
    store_vector(flat, "norm_gain", sums[0])
    store_vector(flat, "norm_shift", sums[1])


def narrow(flat, low, first, last, base):
    block = 256

    def part(index, size):
        at = first + index * block
        source = pl.ds(pl.multiple_of(at, TILE), size)
        low[pl.ds(pl.multiple_of(at - base, TILE), size), :] = flat[source, :].astype(BF)

    loop((last - first) // block, lambda index: part(index, block))
    if (last - first) % block:
        part((last - first) // block, (last - first) % block)


def flat_from_slots(count, shard, small, slots, flat, widened=False):
    size = shard // UNIT * TILE

    def tile_of(index):
        return index * shard // UNIT * TILE

    def slot(index, row, rows):
        at = pl.ds(pl.multiple_of(index * small + row, TILE), rows)
        return slots[at, :].astype(F32)

    def widen(index):
        at = pl.ds(pl.multiple_of(tile_of(index) + TILE, TILE), size)
        flat[at, :] = slot(index, TILE, size)

    if not widened:
        return widen
    flat[0:TILE, :] = slot(0, 0, TILE)

    def edge(index):
        place = tile_of(index + 1)
        tail = slot(index, place - tile_of(index), TILE)
        flat[pl.ds(pl.multiple_of(place, TILE), TILE), :] = tail + slot(index + 1, 0, TILE)

    loop(count - 1, edge)
    last = tile_of(count)
    flat[last : last + TILE, :] = slot(count - 1, last - tile_of(count - 1), TILE)


def divide(value, by):
    return lax.div(value, lax.full_like(value, by))


def rest_of(value, by):
    return lax.rem(value, lax.full_like(value, by))


class Ring:
    def __init__(self, images, rows):
        self.side = side = math.isqrt(images // 2)
        assert 2 * side * side == images
        self.images, self.rows = images, rows
        self.img = lax.axis_index("img")
        self.row = lax.axis_index("row")
        self.core = rest_of(self.img, 2)
        place = divide(self.img, 2)
        a, b = divide(place, side), rest_of(place, side)
        one = self.core == 1
        self.u = jnp.where(one, a, b)
        self.w = jnp.where(one, b, a)
        self.us = [rest_of(self.u + o, side) for o in range(side)]
        self.ws = [rest_of(self.w + o, side) for o in range(side)]
        first_step = jnp.where(one, 2 * side, 2)
        second_step = jnp.where(one, 2, 2 * side)
        self.images_at = {
            (i, j): u * first_step + w * second_step + self.core
            for i, u in enumerate(self.us)
            for j, w in enumerate(self.ws)
        }
        self.row_at = [rest_of(self.row + o, rows) for o in range(rows)]
        self.near = [self.nearest(k) for k in range(rows)]
        self.other = self.img + 1 - 2 * self.core

    def image(self, i, j):
        return self.images_at[i % self.side, j % self.side]

    def along_row(self, o):
        return (self.img, self.row_at[o % self.rows])

    def nearest(self, k):
        if k == 0:
            return self.row
        row, last = self.row, self.rows - 1
        inside = row - (k + 1) // 2 if k % 2 else row + k // 2
        outside = jnp.where(row < last - row, k, last - k)
        return jnp.where(k <= 2 * jnp.minimum(row, last - row), inside, outside)

    def rank(self, row, other):
        last = self.rows - 1
        inside = jnp.where(other < row, 2 * (row - other) - 1, 2 * (other - row))
        outside = jnp.where(row < last - row, other, last - other)
        apart = jnp.maximum(row - other, other - row)
        return jnp.where(apart <= jnp.minimum(row, last - row), inside, outside)

    def along_first(self, o):
        return (self.image(o, 0), self.row)

    def along_second(self, o):
        return (self.image(0, o), self.row)

    def sibling(self):
        return (self.other, self.row)

    def partners(self):
        out = [self.along_row(o) for o in range(1, self.rows)]
        out += [self.along_first(o) for o in range(1, self.side)]
        out += [self.along_second(o) for o in range(1, self.side)]
        return out + [self.sibling()]

    def signal(self, semaphore):
        for partner in self.partners():
            pl.semaphore_signal(semaphore, inc=1, device_id=partner, device_id_type=MESH)

    def wait(self, semaphore):
        pl.semaphore_wait(semaphore, self.rows - 1 + 2 * (self.side - 1) + 1)


class Transfer:
    def __init__(self, ring, send, recv):
        self.ring, self.send, self.recv = ring, send, recv
        self.started = []

    def start(self, index, source, target, device, recv=None, when=None):
        def make():
            return pltpu.make_async_remote_copy(
                src_ref=source(),
                dst_ref=target(),
                send_sem=self.send.at[index],
                recv_sem=self.recv.at[index if recv is None else recv],
                device_id=device,
                device_id_type=MESH,
            )

        def run(act):
            if when is None:
                act()
            else:
                pl.when(when)(act)

        run(lambda: make().start())
        self.started.append(lambda: run(lambda: make().wait_send()))

    def arrived(self, index, target):
        pltpu.make_async_remote_copy(
            src_ref=target,
            dst_ref=target,
            send_sem=self.send.at[index],
            recv_sem=self.recv.at[index],
            device_id=self.ring.sibling(),
            device_id_type=MESH,
        ).wait_recv()

    def sent(self):
        for wait in self.started:
            wait()
        self.started = []


def gather_count(images, rows):
    side = math.isqrt(images // 2)
    return rows + 1 + rows * (side - 1) * (1 + side) + rows * side * side


class Gather(Transfer):
    def __init__(self, ring, own, slots, small, send, recv, local, single=False):
        super().__init__(ring, send, recv)
        self.single = single
        self.own, self.slots, self.small, self.local = own, slots, small, local
        rows, side = ring.rows, ring.side
        self.first_at = rows + 1
        self.second_at = self.first_at + (side - 1) * rows
        self.near_at = self.second_at + (side - 1) * side * rows
        images = {(q, o2): ring.image(-q, -o2) for q in range(side) for o2 in range(side)}
        self.blocks = {at: image * (rows * small) for at, image in images.items()}
        self.places = {
            (*at, k): block + ring.near[k] * small
            for at, block in self.blocks.items()
            for k in range(rows)
        }
        self.ranks = [ring.rank(ring.near[k], ring.row) - 1 for k in range(rows)]

    def block(self, q, o2):
        size = self.ring.rows * self.small
        return self.slots.at[pl.ds(pl.multiple_of(self.blocks[q, o2], TILE), size), :]

    def here(self, q, o2, k):
        start = pl.multiple_of(self.places[q, o2, k], TILE)
        return self.slots.at[pl.ds(start, self.small), :]

    def pass_on(self, source, q, o2, k):
        ring = self.ring
        rows, side = ring.rows, ring.side

        def target():
            return self.here(q, o2, k)

        if q == 0 and o2 == 0:
            for o in range(1, side):
                self.start(
                    self.first_at + (o - 1) * rows + k,
                    source,
                    target,
                    ring.along_first(o),
                )
        if o2 == 0:
            for o in range(1, side):
                self.start(
                    self.second_at + ((o - 1) * side + q) * rows + k,
                    source,
                    target,
                    ring.along_second(o),
                )
        if self.single:
            near = self.near_at + (o2 * side + q) * rows + k
            self.start(near, source, target, ring.sibling())
        elif k == rows - 1:
            if q == 0 and o2 == 0:
                pltpu.make_async_copy(self.own, self.here(0, 0, 0), self.local).wait()
            block = functools.partial(self.block, q, o2)
            self.start(self.near_at + o2 * side + q, block, block, ring.sibling())

    def begin(self):
        ring = self.ring

        def own():
            return self.own

        for k in range(1, ring.rows):
            self.start(
                k - 1,
                own,
                lambda: self.here(0, 0, 0),
                (ring.img, ring.near[k]),
                recv=self.ranks[k],
            )
        self.pass_on(own, 0, 0, 0)
        pltpu.make_async_copy(self.own, self.here(0, 0, 0), self.local).start()

    def arrivals(self):
        rows, side = self.ring.rows, self.ring.side
        arrivals = []
        for k in range(rows):
            if k:
                arrivals.append((k, 0, k - 1, (0, 0, k)))
            for o in range(1, side):
                arrivals.append((k + 1, 1, self.first_at + (o - 1) * rows + k, (o, 0, k)))
                for q in range(side):
                    index = self.second_at + ((o - 1) * side + q) * rows + k
                    arrivals.append((k + 1 + (q > 0), 2, index, (q, o, k)))
        arrivals.sort(key=lambda item: item[:2])
        return [(index, place) for _, _, index, place in arrivals]

    def step(self, index, place):
        self.arrived(index, self.here(*place))
        self.pass_on(lambda: self.here(*place), *place)

    def steps(self):
        arrivals = self.arrivals()
        first, per = 5.5, 25.0 / len(arrivals)
        return [
            (first + per * n, functools.partial(self.step, index, place))
            for n, (index, place) in enumerate(arrivals)
        ]

    def finish(self):
        ring = self.ring
        for index in range(self.near_at, self.near_at + ring.side * ring.side):
            self.arrived(index, self.block(0, 0))
        self.sent()

    def all_single(self, here):
        ring = self.ring
        steps = self.arrivals()
        for index, (q, o2, k) in steps:
            self.step(index, (q, o2, k))
            here(ring.image(-q, -o2), ring.near[k])
        pltpu.make_async_copy(self.own, self.here(0, 0, 0), self.local).wait()
        here(ring.img, ring.row)
        yield
        order = sorted(
            ((o2, q, k) for o2 in range(ring.side) for q in range(ring.side) for k in range(ring.rows)),
            key=lambda at: at[2] + (at[0] > 0) + (at[1] > 0),
        )
        for o2, q, k in order:
            self.arrived(self.near_at + (o2 * ring.side + q) * ring.rows + k, self.here(0, 0, 0))
            here(ring.image(-o2, -q) + 1 - 2 * ring.core, ring.near[k])
        self.sent()


def add_rows(count, size, target, sources):
    def part(at):
        total = None
        for source in sources:
            value = source(at).astype(F32)
            total = value if total is None else total + value
        target(at, total)

    block = max(TILE, min(LANES, 256 // count))
    loop(size // block, lambda index: part(pl.ds(pl.multiple_of(index * block, TILE), block)))
    if size % block:
        part(pl.ds(size // block * block, size % block))


def shifted(at, start):
    return pl.ds(pl.multiple_of(at.start + start, TILE), at.size)


class Sums(Transfer):
    def __init__(self, ring, source, span, shard, buffers, turn, send, recv, base=0):
        super().__init__(ring, send, recv)
        self.source, self.span, self.shard, self.base = source, span, shard, base
        self.lo, self.hi, self.count, self.size = span.lo, span.hi, span.count, span.size
        self.near, self.one, self.two, self.last, self.own, self.inbox = buffers
        self.turn, self.flat_size = turn, span.count * span.size
        self.line = ring.rows * self.size
        self.plane = ring.side * self.line
        self.half = ring.side * self.plane
        self.first_at = ring.side
        self.last_at = self.first_at + ring.side - 1
        self.owner_at = self.last_at + ring.rows - 1
        self.slots = self.inbox.shape[0]
        self.me = ((ring.core * ring.side + ring.w) * ring.side + ring.u) * ring.rows + ring.row
        self.device = ring.img * ring.rows + ring.row
        self.devices = ring.images * ring.rows
        self.mine = base + ring.core * self.half
        self.theirs = base + (1 - ring.core) * self.half
        self.planes = [w * self.plane for w in ring.ws]
        self.lines = [u * self.line for u in ring.us]
        self.places = [
            self.planes[0] + self.lines[0] + row * self.size for row in ring.row_at
        ]
        self.targets = [
            (divide(owner, ring.rows), rest_of(owner, ring.rows), here, self.slot(owner))
            for owner, here in self.owners()
        ]
        self.receives = [self.owner_at + slot for _, _, _, slot in self.targets]
        self.low, self.high = self.range_of(self.device)

    @staticmethod
    def scratch(images, rows, shard, span):
        side, n, size = math.isqrt(images // 2), span.count, span.size
        slots = Sums.slots_of(shard, span)
        return (
            ((n, side * side * rows * size, LANES), BF),
            ((side - 1, n, side * rows * size, LANES), BF),
            ((side - 1, n, rows * size, LANES), BF),
            ((rows - 1, n, size, LANES), BF),
            ((n * size, LANES), BF),
            ((slots, n * size, LANES), BF),
        )

    @staticmethod
    def slots_of(shard, span):
        if span.tiles:
            return len(span.tiles)
        return -(-(shard // LANES + 2) // (span.count * span.size)) + 1

    @staticmethod
    def number(images, rows, shard, span):
        side = math.isqrt(images // 2)
        return 1 + 2 * (side - 1) + rows - 1 + Sums.slots_of(shard, span) + 2

    def cut(self, ref, start, size):
        return ref.at[:, pl.ds(pl.multiple_of(start, TILE), size), :]

    def add(self, start, size, others):
        base = self.mine + start

        def keep(at, total):
            self.near[:, shifted(at, start), :] = total.astype(BF)

        terms = [
            lambda at: self.source[:, shifted(at, base), :],
            lambda at: self.near[:, shifted(at, start), :],
        ]
        add_rows(self.count, size, keep, terms + others)

    def begin(self):
        self.start(
            0,
            lambda: self.cut(self.source, self.theirs, self.half),
            lambda: self.near,
            self.ring.sibling(),
        )

    def second(self):
        ring = self.ring
        self.arrived(0, self.near)
        for j in range(1, ring.side):
            self.add(self.planes[j], self.plane, [])
            self.start(
                j,
                lambda j=j: self.cut(self.near, self.planes[j], self.plane),
                lambda j=j: self.one.at[j - 1],
                ring.along_second(j),
            )

    def across(self, place):
        return [
            lambda at, j=j: self.one[j - 1, :, shifted(at, place), :]
            for j in range(1, self.ring.side)
        ]

    def first(self):
        ring = self.ring
        for j in range(1, ring.side):
            self.arrived(j, self.one.at[j - 1])
        for i in range(1, ring.side):
            start = self.planes[0] + self.lines[i]
            self.add(start, self.line, self.across(self.lines[i]))
            self.start(
                self.first_at + i - 1,
                lambda i=i: self.cut(self.near, self.planes[0] + self.lines[i], self.line),
                lambda i=i: self.two.at[i - 1],
                ring.along_first(i),
            )

    def row(self):
        ring = self.ring
        terms = self.across(self.lines[0])
        for i in range(1, ring.side):
            self.arrived(self.first_at + i - 1, self.two.at[i - 1])
            terms.append(lambda at, i=i: self.two[i - 1, :, at, :])
        self.add(self.planes[0] + self.lines[0], self.line, terms)
        for o in range(1, ring.rows):
            self.start(
                self.last_at + o - 1,
                lambda o=o: self.cut(self.near, self.places[o], self.size),
                lambda o=o: self.last.at[o - 1],
                ring.along_row(o),
            )

    def row_of(self, piece):
        if self.span.tiles:
            plain = len(self.span.tiles) - 6
            valid = jnp.where(piece < plain, TILE, 0)
            out = (self.span.tiles[0][1] + piece * TILE, 0, valid)
            for index, (_, row, first, end) in list(enumerate(self.span.tiles))[plain:]:
                out = tuple(
                    jnp.where(piece == index, new, old) for new, old in zip((row, first, end), out)
                )
            return out
        row = self.lo + piece * self.flat_size
        return row, 0, jnp.minimum(self.hi - row, self.flat_size)

    def range_of(self, owner):
        first = divide(owner * self.shard, LANES) - self.lo
        last = divide((owner + 1) * self.shard - 1, LANES)
        last = jnp.minimum(last, self.hi - 1) - self.lo
        low = divide(jnp.maximum(first, 0), self.flat_size)
        high = divide(jnp.maximum(last + self.flat_size, 0), self.flat_size) - 1
        return low, jnp.minimum(high, self.devices - 1)

    def slot(self, owner):
        return self.me if self.span.tiles else jnp.maximum(self.me - self.range_of(owner)[0], 0)

    def owners(self):
        row, begin, end = self.row_of(self.me)
        there = end > begin
        first = jnp.minimum(divide((row + begin) * LANES, self.shard), self.devices - 1)
        last = divide(jnp.maximum((row + end) * LANES - 1, 0), self.shard)
        last = jnp.minimum(last, self.devices - 1)
        return (
            (first, there & (first != self.device)),
            (last, there & (last > first) & (last != self.device)),
        )

    def final(self):
        ring = self.ring
        terms = [lambda at: self.near[:, shifted(at, self.places[0]), :]]
        for o in range(1, ring.rows):
            self.arrived(self.last_at + o - 1, self.last.at[o - 1])
            terms.append(lambda at, o=o: self.last[o - 1, :, at, :])

        def keep(at, total):
            if self.count == 1:
                self.turn[at, :] = total[0]
                return
            for tile in range(self.count):
                first = at.start * self.count + tile
                self.turn[pl.ds(first, at.size, stride=self.count), :] = total[tile]

        add_rows(self.count, self.size, keep, terms)
        self.own[...] = self.turn[: self.flat_size, :].astype(BF)
        for t, (image, row, here, slot) in enumerate(self.targets):
            self.start(
                self.owner_at + self.slots + t,
                lambda: self.own,
                lambda slot=slot: self.inbox.at[slot],
                (image, row),
                recv=self.receives[t],
                when=here,
            )

    def collect(self, target, margin):
        low, high = self.low, self.high
        for t in range(self.slots):
            if self.span.tiles:
                _, row, begin, end = self.span.tiles[t]
                first = (row + begin) * LANES // self.shard
                last = ((row + end) * LANES - 1) // self.shard
                here, piece = (self.device >= first) & (self.device <= last), t
            else:
                here, piece = low + t <= high, low + t
                row, begin, end = self.row_of(piece)

            @pl.when(here)
            def _(t=t, piece=piece, row=row, begin=begin, end=end):
                mine = piece == self.me

                @pl.when(mine)
                def _():
                    self.inbox[t] = self.own[...]

                @pl.when(jnp.logical_not(mine))
                def _():
                    self.arrived(self.owner_at + t, self.inbox.at[t])

                start = row - divide(self.device * self.shard, UNIT) * TILE + margin
                if not self.span.tiles and self.lo % 8 == 0 and self.flat_size % 8 == 0:
                    start = pl.multiple_of(start, 8)
                if self.span.tiles:
                    start = pl.multiple_of(start, TILE)
                at = pl.ds(start, self.flat_size)
                index = lax.broadcasted_iota(jnp.int32, (self.flat_size, LANES), 0)
                target[at, :] = jnp.where(
                    (index >= begin) & (index < end), self.inbox[t].astype(F32), target[at, :]
                )

    def steps(self, target, margin, pace, delay=0.0, halo=0.0):
        unit = self.flat_size * LANES * 2 / pace[0]
        hop, out, time = pace[1], [], 0.0
        for step, after in (
            (self.begin, 16 * unit / 6),
            (self.second, 8 * unit),
            (self.first, 4 * unit),
            (self.row, 8 * unit),
            (self.final, 3 * unit + 2.0),
        ):
            if step == self.row:
                time = max(time, halo)
            out.append((time, step))
            time += after + hop
            if step == self.begin:
                time += delay

        def collect():
            self.collect(target, margin)

        collect.ends = True
        return out + [(time + 2 * hop, collect)]


class Halo(Transfer):
    def __init__(self, ring, grid, source, above, below, send, recv, first=0, width=None):
        super().__init__(ring, send, recv)
        columns = pl.ds(first, source.shape[1] if width is None else width)
        above, below = above.at[:, columns], below.at[:, columns]
        self.has_above, self.has_below = ring.row > 0, ring.row < ring.rows - 1
        self.above, self.below = above, below
        halo, pixels = grid.halo, grid.pixels
        self.moves = (
            (0, source.at[pl.ds(pixels - halo, halo), columns], above, 1, self.has_below, self.has_above),
            (1, source.at[pl.ds(0, halo), columns], below, ring.rows - 1, self.has_above, self.has_below),
        )

    def make(self, index, source, target, o):
        return pltpu.make_async_remote_copy(
            src_ref=source,
            dst_ref=target,
            send_sem=self.send.at[index],
            recv_sem=self.recv.at[index],
            device_id=self.ring.along_row(o),
            device_id_type=MESH,
        )

    def begin(self):
        for index, source, target, o, sends, gets in self.moves:

            @pl.when(sends)
            def _():
                self.make(index, source, target, o).start()

            @pl.when(jnp.logical_not(gets))
            def _():
                target[...] = jnp.zeros(target.shape, target.dtype)

    def finish(self):
        for index, source, target, o, sends, gets in self.moves:

            @pl.when(gets)
            def _():
                self.make(index, source, target, o).wait_recv()

            @pl.when(sends)
            def _():
                self.make(index, source, target, o).wait_send()


def call(kernel, identity, ins, outs, scratch, sems, limits, fetched=(), spilled=(), placed=None):
    placed = placed or {}
    fetch = {k: v for group in fetched for k, v in group.items()}
    spill = {k: v for group in spilled for k, v in group.items()}
    names = list(ins) + list(limits) + list(fetch) + list(outs) + list(spill) + list(placed)
    direct = set(ins) | set(limits) | set(outs) | set(placed)
    buffers = {k: (v.shape, v.dtype) for k, v in fetch.items()}
    buffers.update({k: v for k, v in spill.items() if k not in scratch})
    buffers.update(scratch)
    counts = dict(sems, fetch_sem=max(len(fetch), 1), spill_sem=max(len(spill), 1))

    def run(*refs):
        given = dict(zip(names, refs))
        rest = dict(zip(list(buffers) + list(counts) + [CREDIT], refs[len(names) :]))
        r = SimpleNamespace(**{k: v for k, v in given.items() if k in direct})
        for k, v in rest.items():
            setattr(r, k, v)
        groups = [list(group) for group in fetched]
        copies = {
            k: pltpu.make_async_copy(given[k], rest[k], r.fetch_sem.at[i])
            for i, k in enumerate(fetch)
        }
        for copy in copies.values():
            copy.start()

        def needed():
            if groups:
                for k in groups.pop(0):
                    copies[k].wait()

        leaving = [list(group) for group in spilled]
        gone, started = [], []

        def written():
            if leaving:
                for k in leaving.pop(0):
                    copy = pltpu.make_async_copy(
                        getattr(r, k), given[k], r.spill_sem.at[len(started)]
                    )
                    started.append(k)
                    copy.start()
                    gone.append(copy)

        def settled():
            while gone:
                gone.pop().wait()

        r.needed, r.written, r.settled = needed, written, settled
        kernel(r)
        while leaving:
            written()
        while groups:
            needed()
        settled()

    vmem = pl.BlockSpec(memory_space=pltpu.VMEM)
    smem = pl.BlockSpec(memory_space=pltpu.SMEM)
    anywhere = pl.BlockSpec(memory_space=pl.ANY)
    shapes = list(outs.values()) + list(spill.values()) + list(placed.values())
    results = pl.pallas_call(
        run,
        out_shape=[jax.ShapeDtypeStruct(*shape) for shape in shapes],
        in_specs=[vmem] * len(ins) + [smem] * len(limits) + [anywhere] * len(fetch),
        out_specs=[vmem] * len(outs) + [anywhere] * (len(spill) + len(placed)),
        scratch_shapes=[pltpu.VMEM(*shape) for shape in buffers.values()]
        + [
            pltpu.SemaphoreType.DMA(count if isinstance(count, tuple) else (count,))
            for count in counts.values()
        ]
        + [pltpu.SemaphoreType.REGULAR],
        compiler_params=pltpu.CompilerParams(
            collective_id=identity, has_side_effects=True, vmem_limit_bytes=VMEM_LIMIT
        ),
    )(*ins.values(), *limits.values(), *fetch.values())
    return SimpleNamespace(**dict(zip(names[len(ins) + len(limits) + len(fetch) :], results)))


def fill_mask(grid, row, heights, widths, mask, first, count):
    col = lax.broadcasted_iota(jnp.int32, (grid.cols, LANES), 0)
    for index in range(count):
        line = jnp.full((grid.cols, LANES), row * grid.rows + first + index, jnp.int32)
        valid = (line >= 0) & (line < heights[0]) & (col < widths[0])
        mask[index * grid.cols : (index + 1) * grid.cols, :] = jnp.where(valid, 1.0, 0.0)


def align_in(start, small, raw, own, flat, layer):
    shift, down = start % LANES, start // LANES % TILE
    low = lax.broadcasted_iota(jnp.int32, (small, LANES), 1) < shift
    count, second = raw.shape[1], 2048
    flat[0:8, :] = jnp.zeros((8, LANES), F32)
    flat[8 : 8 + count, :] = raw[layer].astype(F32)
    flat[8 + count : 40 + count, :] = jnp.zeros((32, LANES), F32)
    before = pltpu.roll(flat[7 : 7 + small, :], shift, 1)
    here = pltpu.roll(flat[8 : 8 + small, :], shift, 1)
    flat[second : second + TILE, :] = jnp.zeros((TILE, LANES), F32)
    flat[pl.ds(second + down, small), :] = jnp.where(low, before, here)
    own[layer] = flat[second : second + small, :].astype(BF)


def align_out(start, margin, summed, result, layer):
    shift, down = start % LANES, start // LANES % TILE + margin
    count = result.shape[1]
    low = lax.broadcasted_iota(jnp.int32, (count, LANES), 1) < LANES - shift
    back = (LANES - shift) % LANES
    here = pltpu.roll(summed[layer, pl.ds(down, count), :], back, 1)
    after = pltpu.roll(summed[layer, pl.ds(down + 1, count), :], back, 1)
    result[layer] = jnp.where(low, here, after)


def body(images, cotangent, params, heights, widths):
    grid = Grid(images.shape[1], images.shape[2])
    depth, shard = params.shape
    image_count, row_count = lax.axis_size("img"), lax.axis_size("row")
    count = image_count * row_count
    pixels, width = grid.pixels, images.shape[3]

    small = (shard // UNIT + 2) * TILE
    chunks = -(-shard // UNIT) * TILE
    raw = jnp.pad(params, ((0, 0), (0, chunks * LANES - shard))).reshape(depth, chunks, LANES)

    def parted(stage, first, end, parts=1):
        size = -(-(end - first) // (parts * count * TILE)) * TILE
        return [
            SimpleNamespace(
                stage=stage, name=None, tiles=None, count=1, size=size, lo=start,
                hi=min(start + count * size, end), base=0, start=start,
            )
            for start in range(first, end, count * size)
        ]

    def wire(stage, name, part=0, parts=1):
        start, (rows, columns) = CHUNK[name]
        tiles, rows = columns // LANES, rows // parts
        start += part * rows * tiles
        return SimpleNamespace(
            stage=stage, name=name, tiles=None, count=tiles, size=rows // count, lo=start,
            hi=start + rows * tiles, base=part * rows, start=0,
        )

    wired = all(CHUNK[name][1][0] % (TILE * count) == 0 for name in WIRED)
    if wired:
        spans = [wire(1, WIRED[0]), wire(1, WIRED[1])] + parted(2, PART, GATES_END)
        spans.append(wire(3, WIRED[2]))
        spans.append(
            SimpleNamespace(
                stage=4, name=None, tiles=TILES, count=1, size=TILE, lo=0, hi=0, base=0, start=0
            )
        )
    else:
        spans = parted(1, MIDDLE, BODY_ROWS, 2) + parted(2, PART, MIDDLE) + parted(4, 0, PART)
    margin = max(span.count * span.size for span in spans) + TILE
    sources, shapes, of_name = {}, [], {}
    for index, span in enumerate(spans):
        shapes.append(((span.count, count * span.size, LANES), BF))
        if span.name:
            rows = CHUNK[span.name][1][0]
            of_name[span.name] = SOURCE.format(span.name)
            sources[of_name[span.name]] = ((span.count, rows, LANES), BF)
        elif wired:
            sources[SOURCE.format(index)] = shapes[-1]
    flat_rows = 0 if wired else max(span.lo + count * span.size for span in spans)
    slots_rows = max(flat_rows, count * small)

    def source_of(r, index):
        span = spans[index]
        if span.name:
            return getattr(r, of_name[span.name])
        if wired:
            return getattr(r, SOURCE.format(index))
        return r.slots.at[:, pl.ds(span.start, count * span.size), :]

    late = [
        index for index, span in enumerate(spans) if span.stage >= 3 or span.name == WIRED[1]
    ]

    slots_shape = ((1, slots_rows, LANES), BF)
    field = ((grid.tall * grid.wide * 8, LANES), F32)
    wide = ((pixels, width), F32)
    low = ((pixels, width), BF)
    broad = ((pixels, 4 * width), BF)
    inner = ((pixels, 2 * width), BF)
    narrow_tile = ((pixels, LANES), F32)
    registers = ((pixels * 8, LANES), F32)
    taps = ((49 * 8, LANES), F32)
    taps_grad = ((50 * 8, LANES), F32)
    flat = ((BODY_ROWS, LANES), F32)
    halo = ((grid.halo, width), BF)
    halo_wide = ((grid.halo, 2 * width), BF)
    mask = ((grid.all, LANES), F32)
    own_mask = ((pixels, LANES), F32)
    sum_shape = ((small + 2 * margin, LANES), F32)
    vectors = ((24, 4 * width), F32)
    weights = {name: (PADDED[name], BF) for name in MATRICES}
    kept_one = dict(weights, vectors=vectors, taps=taps, normed=low, field=field)
    kept_two = dict(
        mixed=registers, head=narrow_tile, lines=((pixels, 896), BF), gated=inner,
        branch_a=low, middle=wide, normed_b=low,
    )
    kept_three = dict(active=broad, slope=broad)
    kept_four = dict(branch_b=low)
    front_scratch = dict(
        flat=flat, normed_all=((grid.all, width), BF),
        bias=((8, LANES), F32), x_up=halo, x_down=halo, mask=mask,
    )
    back_scratch = dict(
        grad_up=halo_wide, grad_down=halo_wide, low=low, wide=wide, taps_grad=taps_grad,
        turned=((width, pixels), BF),
    )
    pieces = gather_count(image_count, row_count)
    side = math.isqrt(image_count // 2)
    sum_scratch, sum_sems = {}, {}
    for again, indices in enumerate((range(len(spans)), late)):
        for index in indices:
            parts = Sums.scratch(image_count, row_count, shard, spans[index])
            sum_scratch.update(
                {SUMS.format(index, again, at): shape for at, shape in enumerate(parts)}
            )
            number = Sums.number(image_count, row_count, shard, spans[index])
            sum_sems.update(
                {SENDS.format(index, again): number, RECEIVES.format(index, again): number}
            )
    once = {k: v for k, v in sum_scratch.items() if k.split(DASH)[2] == str(0)}
    once_sems = {k: v for k, v in sum_sems.items() if k.split(DASH)[2] == str(0)}
    turn = ((margin, LANES), F32)

    def summing(r, ring, index, again=0):
        parts = [getattr(r, SUMS.format(index, again, at)) for at in range(6)]
        send = getattr(r, SENDS.format(index, again))
        recv = getattr(r, RECEIVES.format(index, again))
        source = getattr(r, BEFORE.format(index)) if again else source_of(r, index)
        return Sums(ring, source, spans[index], shard, parts, r.turn, send, recv, spans[index].base)

    def wires_of(r):
        return {name: getattr(r, source) for name, source in of_name.items()}

    def settle(r, stage):
        for index, span in enumerate(spans):
            if span.stage == stage and not span.name:
                low = source_of(r, index).at[0]
                if span.tiles:
                    for at, (row, _, _, _) in enumerate(span.tiles):
                        low[at * TILE : (at + 1) * TILE, :] = r.flat[row : row + TILE, :].astype(BF)
                else:
                    narrow(r.flat, low, span.lo, -(-span.hi // TILE) * TILE, span.lo)

    def known(r, ring, beside, stage, target, sums, leave=()):
        settle(r, stage)
        delay, halo = 0.0, (23.5, 19.5, 12.0, 0.0, 0.0)[stage]
        for index, span in enumerate(spans):
            if span.stage == stage and index not in leave:
                part = summing(r, ring, index)
                beside.add(part.steps(target, margin, beside.pace, delay, halo))
                delay += 8 * span.count * span.size * LANES * 2 / beside.pace[0]
                sums.append(part)
        beside.tick(0.0)

    x = images.reshape(pixels, width)
    limits = dict(heights=heights, widths=widths)

    def own_rows(ref):
        return ref.at[pl.ds(grid.halo, pixels), :]

    def kernel_ab(r):
        ring = Ring(image_count, row_count)
        ring.signal(pltpu.get_barrier_semaphore())
        shard_at = (ring.img * row_count + ring.row) * shard
        align_in(shard_at, small, r.raw, r.own, r.flat, 0)
        ring.wait(pltpu.get_barrier_semaphore())
        first = Gather(
            ring, r.own.at[0], r.slots.at[0], small, r.send, r.recv, r.local.at[0], single=True
        )
        first.begin()
        halos = Halo(
            ring, grid, r.x, r.x_up, r.x_down, r.halo_send.at[3], r.halo_recv.at[3]
        )
        halos.begin()
        for layer in range(1, depth):
            align_in(shard_at, small, r.raw, r.own, r.flat, layer)
        fill_mask(grid, ring.row, r.heights, r.widths, r.mask, -3, grid.tall)
        widen = flat_from_slots(count, shard, small, r.slots.at[0], r.flat)
        rest = first.all_single(lambda image, row: widen(image * row_count + row))
        next(rest)
        second = Gather(ring, r.own.at[1], r.slots_b.at[0], small, r.send_b, r.recv_b, r.local.at[1])
        second.begin()
        next(rest, None)
        beside = Steps()
        beside.add(second.steps())
        flat_from_slots(count, shard, small, r.slots.at[0], r.flat, True)
        beside.tick(0.5)
        weights_from_flat(r.flat, r, r.vectors, r.taps, r.bias, beside)
        r.normed = own_rows(r.normed_all)
        forward(grid, r, Vectors(r.vectors), r.taps, r, beside, halos.finish, r.written)
        r.x1[...] = r.result[...]
        r.low[...] = r.result[...].astype(BF)
        halos = Halo(ring, grid, r.low, r.x1_up, r.x1_down, r.halo_send.at[0], r.halo_recv.at[0])
        halos.begin()
        beside.drain()
        second.finish()
        fetch = pltpu.make_async_copy(r.slots_b, r.slots, r.late_sem.at[len(late)])
        fetch.start()
        r.x, r.x_up, r.x_down = r.x1, r.x1_up, r.x1_down
        r.settled()
        fetch.wait()
        beside = Steps()
        loop(count, flat_from_slots(count, shard, small, r.slots.at[0], r.flat))
        flat_from_slots(count, shard, small, r.slots.at[0], r.flat, True)
        weights_from_flat(r.flat, r, r.vectors, r.taps, r.bias, beside)
        r.normed = own_rows(r.normed_all)
        r.mask_own = own_rows(r.mask)
        v = Vectors(r.vectors)
        r.back = r.result
        forward(grid, r, v, r.taps, r, beside, halos.finish, lambda: None)
        r.outputs[...] = r.result[...].astype(BF)
        sums = []
        r.wires = wires_of(r)
        if wired:
            r.grads = r.flat.at[pl.ds(KEPT_ROWS, field[0][0]), :]

        leaving = []

        def leave(stage):
            for at, index in enumerate(late):
                if (spans[index].stage >= 3) == (stage == 4):
                    copy = pltpu.make_async_copy(
                        source_of(r, index), getattr(r, BEFORE.format(index)), r.late_sem.at[at]
                    )
                    copy.start()
                    leaving.append(copy)

        def at_stage(stage):
            def here():
                known(r, ring, beside, stage, r.summed, sums, late)
                if stage == 1:
                    leave(stage)

            return here

        halos = [
            Halo(
                ring, grid, r.gated, r.grad_up, r.grad_down, r.halo_send.at[at], r.halo_recv.at[at],
                (2 - at) * width, width,
            )
            for at in (1, 2)
        ]
        backward_one(
            grid, r, v, r, r.flat, beside, lambda: None, at_stage(0), at_stage(1), halos[0].begin
        )
        halos[1].begin()
        known(r, ring, beside, 2, r.summed, sums)
        backward_two(
            grid, r, v, r.taps, r, r.flat, beside, lambda: None,
            lambda: [halo.finish() for halo in halos], lambda: None, 7,
        )
        settle(r, 4)
        leave(4)
        beside.drain()
        for part in sums:
            part.sent()
        for copy in leaving:
            copy.wait()

    b = call(
        kernel_ab,
        0,
        dict(raw=raw, x=x, grad=cotangent.reshape(pixels, width)),
        dict(outputs=low, input_grad=wide, summed=sum_shape),
        dict(
            kept_one, **kept_two, **kept_three, **kept_four, **front_scratch, **back_scratch,
            **once, **sources, turn=turn, slots=slots_shape, own=((depth, small, LANES), BF),
            result=wide, x1=wide, x1_up=halo, x1_down=halo, **({} if wired else dict(grads=field)),
        ),
        dict(
            once_sems, send=pieces, recv=pieces, send_b=pieces, recv_b=pieces, local=2,
            halo_send=(4, 2), halo_recv=(4, 2), late_sem=len(late) + 1,
        ),
        limits,
        spilled=(kept_one, kept_two, kept_three, kept_four),
        placed=dict({BEFORE.format(index): shapes[index] for index in late}, slots_b=slots_shape),
    )
    a = b

    def kernel_c(r):
        ring = Ring(image_count, row_count)
        ring.signal(pltpu.get_barrier_semaphore())
        fill_mask(grid, ring.row, r.heights, r.widths, r.mask_own, 0, grid.rows)
        r.both[1] = r.summed[...]
        ring.wait(pltpu.get_barrier_semaphore())
        v = Vectors(r.vectors)
        beside = Steps((LAST_LINK, LAST_HOP))
        r.needed()
        sums = []

        def late_sums(last):
            delay = 0.0
            for index in late[::-1]:
                if (spans[index].stage >= 3) == last:
                    before = summing(r, ring, index, 1)
                    beside.add(before.steps(r.both.at[1], margin, beside.pace, delay))
                    sums.append(before)
                    delay += 4 * spans[index].count * spans[index].size * LANES * 2 / beside.pace[0]
            beside.tick(0.0)

        late_sums(True)
        target = r.both.at[0]
        r.back = r.grad
        r.wires = wires_of(r)

        def at_stage(stage):
            return lambda: known(r, ring, beside, stage, target, sums)

        halos = [
            Halo(
                ring, grid, r.gated, r.grad_up, r.grad_down, r.halo_send.at[at], r.halo_recv.at[at],
                (1 - at) * width, width,
            )
            for at in (0, 1)
        ]

        def half_here():
            r.needed()
            late_sums(False)
            known(r, ring, beside, 0, target, sums)

        backward_one(
            grid, r, v, r, r.flat, beside, r.needed, half_here, at_stage(1), halos[0].begin
        )
        halos[1].begin()
        known(r, ring, beside, 2, target, sums)
        backward_two(
            grid, r, v, r.taps, r, r.flat, beside, r.needed,
            lambda: [halo.finish() for halo in halos], at_stage(3), 4,
        )
        known(r, ring, beside, 4, target, sums)
        start = (ring.img * row_count + ring.row) * shard
        beside.drain(lambda: align_out(start, margin, r.both, r.grads_out, 1))
        align_out(start, margin, r.both, r.grads_out, 0)
        for part in sums:
            part.sent()

    late_parts = [
        {
            BEFORE.format(index): getattr(b, BEFORE.format(index))
            for index in late
            if (spans[index].stage >= 3) == last
        }
        for last in (False, True)
    ]
    c = call(
        kernel_c,
        2,
        dict(x=x, summed=b.summed),
        dict(input_grad=low, grads_out=((depth, chunks, LANES), F32)),
        dict(
            **back_scratch, **sum_scratch, **sources, turn=turn, grads=field,
            flat=((KEPT_ROWS if wired else BODY_ROWS, LANES), F32),
            **({} if wired else dict(slots=((1, flat_rows, LANES), BF))),
            mask_own=own_mask, both=((depth, small + 2 * margin, LANES), F32),
        ),
        dict(sum_sems, halo_send=(2, 2), halo_recv=(2, 2)),
        limits,
        fetched=(
            dict(late_parts[1], grad=b.input_grad, vectors=a.vectors, branch_b=a.branch_b),
            dict(reduce=a.reduce, active=a.active, slope=a.slope, normed_b=a.normed_b),
            late_parts[0],
            dict(expand=a.expand, middle=a.middle, branch_a=a.branch_a),
            dict(outer_weight=a.outer_weight, gated=a.gated, lines=a.lines, mixed=a.mixed, head=a.head,
                 order_one=a.order_one, order_two=a.order_two, order_three=a.order_three),
            dict(field=a.field, taps=a.taps, normed=a.normed, inner_weight=a.inner_weight),
        ),
    )
    summed = c.grads_out.reshape(depth, -1)[:, :shard]
    return (b.outputs.reshape(images.shape), c.input_grad.reshape(images.shape), summed)


def solution(mesh):
    return jax.shard_map(
        body,
        mesh=mesh,
        in_specs=(
            P("img", "row", None, None),
            P("img", "row", None, None),
            P(None, ("img", "row")),
            P("img"),
            P("img"),
        ),
        out_specs=(
            P("img", "row", None, None),
            P("img", "row", None, None),
            P(None, ("img", "row")),
        ),
        check_vma=False,
    )
```
